32 devices in a mesh: lon: 8 (over z, core), lat: 4 (over y, x).
Axes of the slice: x: 2, y: 2, z: 4, core: 2. Of those that a mesh axis runs over, the one named last changes fastest.
Arguments:
- ensemble_prediction: bfloat16 [408, 256, 2048], P(None, 'lat', 'lon'), may hold values from -6 to 6
- mapping_matrix: bfloat16 [96, 408], replicated, may hold values from -0.3125 to 0.3125
- mapping_offset: float32 [96], replicated, may hold values from -3 to 3
- gauge_measured_records: bfloat16 [131072, 256], P(('lon', 'lat')), may hold values from -6 to 6
- gauge_scatter_matrix: bfloat16 [256, 96], replicated, may hold values from -0.375 to 0.375
- gauge_scatter_offset: float32 [96], replicated, may hold values from -3 to 3
- gauge_block_number: int32 [131072, 1], P(('lon', 'lat')), may hold values from 0 to 31; in each aligned block of 4096 rows (0 to 4095, 4096 to 8191, ...) at most 256 rows name the same one
- gauge_point_position: int32 [131072], P(('lon', 'lat')), may hold values from 0 to 16383
- initial_filter_matrix: bfloat16 [96, 96, 3, 3], replicated, may hold values from -0.21875 to 0.21875
- initial_filter_offset: float32 [96], replicated, may hold values from -3 to 3
- latter_filter_matrix: bfloat16 [96, 96, 3, 3], replicated, may hold values from -0.21875 to 0.21875
- latter_filter_offset: float32 [96], replicated, may hold values from -3 to 3
Outputs:
- corrected: bfloat16 [96, 256, 2048], P(None, 'lat', 'lon')
- station_values: bfloat16 [131072, 96], P(('lon', 'lat'))
The draws below stay inside these ranges and needn't reach their ends.
Inputs may be any that keep to these rules, and one draw needn't show every extreme that they name: `gauge_block_number`: among the 4096 rows of one device, at most 256 name the same tile, a bound that some block reaches.
All inputs are finite; a program needn't handle non-finite values.
Results may differ from the reference program's by a relative error of at most 0.01.
Values may be sent and summed in bfloat16 or wider, within the bound.
A program may use at most 192 MiB of HBM per device.

```python
import math
import jax
import jax.numpy as jnp
import numpy as np
from jax import lax

FEATURE_DEPTH = 408
F = 96
OBS = 256
LATC = 64
LONC = 256
STA_DEV = 4096
NORTH_SOUTH_SPAN = 256
EAST_WEST_SPAN = 2048
S = 131072
CAP = 256
N_LAT = 4
DEVICES = 32


def with_ends(entries, stream_key, least, top_value):
    spot = [jax.random.randint(jax.random.fold_in(stream_key, axis), (), 0, length) for axis, length in enumerate(entries.shape)]
    widest = entries.shape.index(max(entries.shape))
    neighbour = spot[:widest] + [(spot[widest] + 1) % entries.shape[widest]] + spot[widest + 1:]
    return entries.at[tuple(spot)].set(least).at[tuple(neighbour)].set(top_value)


def steps_of(own_key, dims, cuts, least, high):
    gain, own = 1.0, jax.random.fold_in(own_key, 6)
    for dim, shards_of in cuts:
        heights = jnp.exp(jax.random.uniform(jax.random.fold_in(own, dim), (shards_of,), jnp.float32, least / len(cuts), high / len(cuts)))
        gain = gain * jnp.repeat(heights, dims[dim] // shards_of).reshape([-1 if axis == dim else 1 for axis in range(len(dims))])
    return gain


def assign_block(rng, own, number, rows, number_of, top, reach, skew):
    order = jax.random.permutation(rng, number_of)
    crowded, usual = load_shares(number_of, rows * top, reach, skew, True), load_shares(number_of, rows * top, reach, skew, False)
    places = jnp.arange(number_of)

    def named(lengths, offset_by):
        used = int((lengths > 0).sum())
        fixed = max(1, used // 4)
        moved = fixed + (places - fixed + offset_by * (used - fixed)) % max(1, number_of - fixed)
        return jnp.zeros((number_of,), jnp.int32).at[order[jnp.where(places < fixed, places, moved)]].set(jnp.asarray(lengths, jnp.int32))

    lengths = jnp.where(number % 4 == 0, named(crowded, number // 4), named(usual, number - number // 4 - 1))
    mixed = jax.random.permutation(jax.random.fold_in(own, 3), number_of)
    giver, sink = mixed[0:number_of // 2 * 2:2], mixed[1:number_of // 2 * 2:2]
    room = jnp.minimum(lengths[giver] - 1, reach - lengths[sink]) // 2
    room = jnp.where((giver == order[0]) | (sink == order[0]) | (lengths[sink] == 0), 0, jnp.maximum(room, 0))
    moved = jax.random.randint(jax.random.fold_in(own, 4), (number_of // 2,), 0, 1 << 20) % (room + 1)
    lengths = lengths.at[giver].add(-moved).at[sink].add(moved)
    items = jnp.searchsorted(jnp.cumsum(lengths), jnp.arange(rows * top), side="right").astype(jnp.int32)
    listing = items.reshape(top, rows).T
    listing = listing[jax.random.permutation(jax.random.fold_in(own, 1), rows)]
    offset_by = jax.random.randint(jax.random.fold_in(own, 2), (rows, 1), 0, top)
    return jnp.take_along_axis(listing, (jnp.arange(top)[None, :] + offset_by) % top, axis=1)


def load_shares(amount, total, bound, slope, full):
    portions = [(1 << 20) // math.isqrt(grade ** slope) + 1 for grade in range(1, amount + 1)]
    largest = bound if full else min(bound, max(-(-total // amount), total * portions[0] // sum(portions)))
    least = 1 if total - largest >= amount - 1 else 0
    given, surplus = [largest] + [least] * (amount - 1), total - largest - least * (amount - 1)
    while surplus > 0:
        movable = [i for i in range(1, amount) if given[i] < largest] or [i for i in range(1, amount) if given[i] < bound]
        mass, left = sum([portions[i] for i in movable]), surplus
        for i in movable:
            extra = min(bound - given[i], max(1, left * portions[i] // mass), surplus)
            given[i] = given[i] + extra
            surplus = surplus - extra
    return np.array(given)


def scatter_about(key, extent, width, reach, pieces=(), kind=jnp.bfloat16):
    array = width * jax.random.normal(key, extent, jnp.float32)
    if pieces:
        array = array * steps_of(key, extent, pieces, -0.22, 0.18)
    return jnp.clip(array, -reach, reach).astype(kind)


def setup_inputs(seed: int = 0) -> dict:
    streams_of = jax.random.split(jax.random.key(seed), 13)
    ensemble_prediction = scatter_about(streams_of[0], (FEATURE_DEPTH, NORTH_SOUTH_SPAN, EAST_WEST_SPAN), 1.0, 6.0, ((1, 4), (2, 8)))
    mapping_matrix = scatter_about(streams_of[1], (F, FEATURE_DEPTH), FEATURE_DEPTH ** -0.5, 0.3125)
    mapping_offset = scatter_about(streams_of[2], (F,), 0.5, 3.0, (), jnp.float32)
    gauge_measured_records = scatter_about(streams_of[3], (S, OBS), 1.0, 6.0, ((0, 32),))
    gauge_scatter_matrix = scatter_about(streams_of[4], (OBS, F), OBS ** -0.5, 0.375)
    gauge_scatter_offset = scatter_about(streams_of[5], (F,), 0.5, 3.0, (), jnp.float32)
    gauge_block_number_keys = jax.random.split(jax.random.fold_in(streams_of[6], 1), S // STA_DEV)
    gauge_block_number_turns = jax.random.permutation(jax.random.fold_in(streams_of[6], 3), S // STA_DEV)
    gauge_block_number = jax.vmap(lambda own, number: assign_block(jax.random.fold_in(streams_of[6], 2), own, number, STA_DEV, DEVICES, 1, CAP, 2))(gauge_block_number_keys, gauge_block_number_turns).reshape((S, 1))
    gauge_point_position = with_ends(jax.random.randint(streams_of[7], (S,), 0, LATC * LONC), jax.random.fold_in(streams_of[7], 1), 0, (LATC * LONC) - 1).astype(jnp.int32)
    initial_filter_matrix = scatter_about(streams_of[8], (F, F, 3, 3), (9 * F) ** -0.5, 0.21875)
    initial_filter_offset = scatter_about(streams_of[9], (F,), 0.5, 3.0, (), jnp.float32)
    latter_filter_matrix = scatter_about(streams_of[10], (F, F, 3, 3), (9 * F) ** -0.5, 0.21875)
    latter_filter_offset = scatter_about(streams_of[11], (F,), 0.5, 3.0, (), jnp.float32)
    return dict(ensemble_prediction=ensemble_prediction, mapping_matrix=mapping_matrix, mapping_offset=mapping_offset, gauge_measured_records=gauge_measured_records, gauge_scatter_matrix=gauge_scatter_matrix, gauge_scatter_offset=gauge_scatter_offset, gauge_block_number=gauge_block_number, gauge_point_position=gauge_point_position, initial_filter_matrix=initial_filter_matrix, initial_filter_offset=initial_filter_offset, latter_filter_matrix=latter_filter_matrix, latter_filter_offset=latter_filter_offset)


def conv_periodic(field, kernel):
    widened = jnp.concatenate([field[:, :, -1:], field, field[:, :, :1]], axis=2)
    widened = jnp.pad(widened, ((0, 0), (1, 1), (0, 0)))
    result = lax.conv_general_dilated(widened.astype(jnp.float32)[None], kernel.astype(jnp.float32), (1, 1), "VALID", dimension_numbers=("NCHW", "OIHW", "NCHW"), precision=lax.Precision.HIGHEST)
    return result[0]


def reference(ensemble_prediction, mapping_matrix, mapping_offset, gauge_measured_records, gauge_scatter_matrix, gauge_scatter_offset, gauge_block_number, gauge_point_position, initial_filter_matrix, initial_filter_offset, latter_filter_matrix, latter_filter_offset):
    mapped_features = jnp.dot(mapping_matrix, ensemble_prediction.reshape(FEATURE_DEPTH, NORTH_SOUTH_SPAN * EAST_WEST_SPAN), preferred_element_type=jnp.float32)
    mapped_features = mapped_features + mapping_offset.astype(jnp.float32)[:, None]
    embedded = (jnp.dot(gauge_measured_records, gauge_scatter_matrix, preferred_element_type=jnp.float32) + gauge_scatter_offset.astype(jnp.float32)[None, :]).astype(jnp.bfloat16)
    tile_index = gauge_block_number[:, 0].astype(jnp.int32)
    lon_index = tile_index // N_LAT
    lat_index = tile_index % N_LAT
    grid_row = lat_index * LATC + gauge_point_position // LONC
    grid_col = lon_index * LONC + gauge_point_position % LONC
    global_cell = (grid_row * EAST_WEST_SPAN + grid_col).astype(jnp.int32)
    merged_sum = mapped_features.at[:, global_cell].add(embedded.astype(jnp.float32).T)
    merged = merged_sum.astype(jnp.bfloat16).reshape(F, NORTH_SOUTH_SPAN, EAST_WEST_SPAN)
    hidden = jax.nn.gelu(conv_periodic(merged, initial_filter_matrix) + initial_filter_offset.astype(jnp.float32)[:, None, None]).astype(jnp.bfloat16)
    corrected = (merged.astype(jnp.float32) + conv_periodic(hidden, latter_filter_matrix) + latter_filter_offset.astype(jnp.float32)[:, None, None]).astype(jnp.bfloat16)
    station_values = corrected.reshape(F, NORTH_SOUTH_SPAN * EAST_WEST_SPAN)[:, global_cell].T
    return corrected, station_values
```

```python
import functools

import jax
import jax.numpy as jnp
from jax import lax
from jax.experimental import pallas as pl
from jax.experimental.pallas import tpu as pltpu
from jax.sharding import PartitionSpec as P

LANES = 128
EDGE = 16
VMEM_BYTES = 56 * 1024 * 1024

VMEM = pl.BlockSpec(memory_space=pltpu.VMEM)
SMEM = pl.BlockSpec(memory_space=pltpu.SMEM)


def params():
    return pltpu.CompilerParams(vmem_limit_bytes=VMEM_BYTES)


def route_kernel(features, columns, pos_ref, cell_ref, rec_ref, w_ref, off_ref, out_ref, emb, slots):
    rows = rec_ref.shape[0]
    total = out_ref.shape[0]

    @pl.loop(0, total // 128)
    def _(b):
        slots[pl.ds(pl.multiple_of(b * 128, 128), 128), :] = jnp.zeros((128, LANES), jnp.float32)

    lane = lax.broadcasted_iota(jnp.int32, (128, LANES), 1)

    @pl.loop(0, rows // 128)
    def _(b):
        at = pl.ds(pl.multiple_of(b * 128, 128), 128)
        e = jnp.dot(rec_ref[at, :], w_ref[...], preferred_element_type=jnp.float32) + off_ref[...]
        e = e.astype(jnp.bfloat16).astype(jnp.float32)
        cell = jnp.broadcast_to(cell_ref[pl.ds(b, 1), :], (128, 128)).T
        line = (cell // columns + 1).astype(jnp.float32)
        place = (cell % columns).astype(jnp.float32)
        e = jnp.where(lane == features, line, jnp.where(lane == features + 1, place, e))
        emb[at, :] = e

    @pl.loop(0, rows // 16)
    def _(b):
        for j in range(16):
            i = b * 16 + j
            slots[pl.ds(pos_ref[i], 1), :] = emb[pl.ds(i, 1), :]

    @pl.loop(0, total // 128)
    def _(b):
        at = pl.ds(pl.multiple_of(b * 128, 128), 128)
        out_ref[at, :] = slots[at, :].astype(jnp.bfloat16)


def merge_kernel(cell_ref, proj_ref, arr_ref, out_ref, rows32, s1, s2, s3, s0):
    total = arr_ref.shape[0]
    cells = proj_ref.shape[0]

    @pl.loop(0, total // 128)
    def _(b):
        at = pl.ds(pl.multiple_of(b * 128, 128), 128)
        rows32[at, :] = arr_ref[at, :].astype(jnp.float32)

    @pl.loop(0, cells // 128)
    def _(b):
        at = pl.ds(pl.multiple_of(b * 128, 128), 128)
        for s in (s0, s1, s2, s3):
            s[at, :] = jnp.zeros((128, LANES), jnp.float32)

    sums = (s0, s1, s2, s3)

    @pl.loop(0, total // 16)
    def _(b):
        for g in range(4):
            idx = [b * 16 + g * 4 + j for j in range(4)]
            at = [pl.ds(cell_ref[i], 1) for i in idx]
            new = [sums[j][at[j], :] + rows32[pl.ds(idx[j], 1), :] for j in range(4)]
            for j in range(4):
                sums[j][at[j], :] = new[j]

    @pl.loop(0, cells // 128)
    def _(b):
        at = pl.ds(pl.multiple_of(b * 128, 128), 128)
        out_ref[at, :] = (
            proj_ref[at, :] + ((s0[at, :] + s1[at, :]) + (s2[at, :] + s3[at, :]))
        ).astype(jnp.bfloat16)


def pair_dot(patches, row, width, w_ref):
    y = None
    for dr in range(4):
        lhs = jnp.concatenate([patches[row + dr, k, pl.ds(0, width), :] for k in range(3)], axis=1)
        part = jnp.dot(lhs, w_ref[pl.ds(dr * 384, 384), :], preferred_element_type=jnp.float32)
        y = part if y is None else y + part
    return y


def conv_kernel(
    features, ends_ref, cell_ref, m_ref, left_ref, right_ref, top_ref, bottom_ref,
    w1_ref, b1_ref, w2_ref, b2_ref, out_ref, got_ref, patches, wide, corr, stage,
):
    height, width, _ = m_ref.shape
    tall = width + EDGE

    def spread(row):
        for k in range(3):
            patches[row, k, :, :] = wide[pl.ds(EDGE - 2 + k, tall), :].astype(jnp.bfloat16)

    for ref, base in ((top_ref, 0), (bottom_ref, height + 2)):
        for t in range(2):
            wide[...] = ref[t].astype(jnp.float32)
            spread(base + t)

    @pl.loop(0, height)
    def _(r):
        wide[pl.ds(0, EDGE), :] = left_ref[r].astype(jnp.float32)
        wide[pl.ds(EDGE, width), :] = m_ref[r].astype(jnp.float32)
        wide[pl.ds(EDGE + width, EDGE), :] = right_ref[r].astype(jnp.float32)
        spread(r + 2)

    @pl.loop(0, height // 2 + 1)
    def _(p):
        y = pair_dot(patches, 2 * p, tall, w1_ref) + b1_ref[...]
        hidden = jax.nn.gelu(y)
        for t in range(2):
            h = 2 * p + t
            outside = ((h == 0) & (ends_ref[0] == 1)) | ((h == height + 1) & (ends_ref[1] == 1))
            part = hidden[:, t * LANES:(t + 1) * LANES]
            wide[pl.ds(0, tall), :] = jnp.where(outside, 0.0, part)
            for k in range(3):
                patches[h, k, pl.ds(0, width), :] = wide[pl.ds(k, width), :].astype(jnp.bfloat16)

    @pl.loop(0, height // 2)
    def _(p):
        y = pair_dot(patches, 2 * p, width, w2_ref) + b2_ref[...]
        for t in range(2):
            r = 2 * p + t
            v = m_ref[r].astype(jnp.float32) + y[:, t * LANES:(t + 1) * LANES]
            corr[pl.ds(pl.multiple_of(r * width, 128), width), :] = v
            out_ref[r] = v.T[:features].astype(jnp.bfloat16)

    total = got_ref.shape[0]

    @pl.loop(0, total // 16)
    def _(b):
        for j in range(16):
            i = b * 16 + j
            stage[pl.ds(i, 1), :] = corr[pl.ds(cell_ref[i], 1), :]

    @pl.loop(0, total // 128)
    def _(b):
        at = pl.ds(pl.multiple_of(b * 128, 128), 128)
        got_ref[at, :] = stage[at, :].astype(jnp.bfloat16)


def return_kernel(features, pos_ref, got_ref, out_ref, rows32, stage):
    total = got_ref.shape[0]
    rows = out_ref.shape[0]

    @pl.loop(0, total // 128)
    def _(b):
        at = pl.ds(pl.multiple_of(b * 128, 128), 128)
        rows32[at, :] = got_ref[at, :].astype(jnp.float32)

    @pl.loop(0, rows // 16)
    def _(b):
        for j in range(16):
            i = b * 16 + j
            stage[pl.ds(i, 1), :] = rows32[pl.ds(pos_ref[i], 1), :]

    @pl.loop(0, rows // 128)
    def _(b):
        at = pl.ds(pl.multiple_of(b * 128, 128), 128)
        out_ref[at, :] = stage[at, :][:, :features].astype(jnp.bfloat16)


def slots_of(tile, devices, capacity):
    block = 128
    hot = (tile.reshape(-1, block)[:, :, None] == jnp.arange(devices, dtype=jnp.int32)).astype(
        jnp.bfloat16
    )
    below = jnp.tril(jnp.ones((block, block), jnp.bfloat16), -1)
    inside = jnp.einsum("ij,bjd->bid", below, hot, preferred_element_type=jnp.float32)
    totals = jnp.sum(hot.astype(jnp.float32), axis=1)
    blocks = totals.shape[0]
    before = jnp.sum(
        jnp.where(
            (jnp.arange(blocks)[:, None] > jnp.arange(blocks)[None, :])[:, :, None],
            totals[None],
            0.0,
        ),
        axis=1,
    )
    rank = jnp.sum((inside + before[:, None, :]) * hot.astype(jnp.float32), axis=2)
    return tile * capacity + rank.reshape(-1).astype(jnp.int32)


def pair_weights(kernel):
    out, into = kernel.shape[:2]
    k = jnp.pad(
        jnp.transpose(kernel, (2, 3, 1, 0)), ((0, 0), (0, 0), (0, LANES - into), (0, LANES - out))
    )
    rest = ((0, 0), (0, 0), (0, 0))
    both = jnp.concatenate(
        [jnp.pad(k, ((0, 1),) + rest), jnp.pad(k, ((1, 0),) + rest)], axis=3
    )
    return both.reshape(4 * 3 * LANES, 2 * LANES)


def pair_bias(bias):
    padded = jnp.pad(bias, (0, LANES - bias.shape[0]))
    return jnp.concatenate([padded, padded])[None]


def on_device(
    ensemble_prediction,
    mapping_matrix,
    mapping_offset,
    gauge_measured_records,
    gauge_scatter_matrix,
    gauge_scatter_offset,
    gauge_block_number,
    gauge_point_position,
    initial_filter_matrix,
    initial_filter_offset,
    latter_filter_matrix,
    latter_filter_offset,
):
    depth, height, width = ensemble_prediction.shape
    features = mapping_matrix.shape[0]
    more = LANES - features
    cells = height * width
    lon_size = lax.axis_size("lon")
    lat_size = lax.axis_size("lat")
    devices = lon_size * lat_size
    held_rows = gauge_measured_records.shape[0]
    capacity = 2 * held_rows // devices
    slot_total = devices * capacity
    f32, bf16 = jnp.float32, jnp.bfloat16

    def exchange(rows):
        return lax.all_to_all(
            rows.reshape(devices, capacity, LANES),
            ("lon", "lat"),
            split_axis=0,
            concat_axis=0,
            tiled=True,
        ).reshape(slot_total, LANES)

    position = slots_of(gauge_block_number[:, 0], devices, capacity)
    payload = pl.pallas_call(
        functools.partial(route_kernel, features, width),
        out_shape=jax.ShapeDtypeStruct((slot_total, LANES), bf16),
        in_specs=[SMEM, VMEM, VMEM, VMEM, VMEM],
        out_specs=VMEM,
        scratch_shapes=[
            pltpu.VMEM((held_rows, LANES), f32),
            pltpu.VMEM((slot_total, LANES), f32),
        ],
        compiler_params=params(),
        name="route",
    )(
        position,
        gauge_point_position.reshape(-1, 128),
        gauge_measured_records,
        jnp.pad(gauge_scatter_matrix, ((0, 0), (0, more))),
        jnp.pad(gauge_scatter_offset, (0, more))[None],
    )
    arrived = exchange(payload)
    line = arrived[:, features].astype(jnp.int32)
    place = arrived[:, features + 1].astype(jnp.int32)
    cell = jnp.clip((line - 1) * width + place, 0, cells - 1)

    projected = lax.dot_general(
        ensemble_prediction.reshape(depth, cells),
        jnp.pad(mapping_matrix, ((0, more), (0, 0))),
        (((0,), (1,)), ((), ())),
        preferred_element_type=f32,
    ) + jnp.pad(mapping_offset, (0, more))[None]

    field = pltpu.VMEM((cells, LANES), f32)
    merged = pl.pallas_call(
        merge_kernel,
        out_shape=jax.ShapeDtypeStruct((cells, LANES), bf16),
        in_specs=[SMEM, VMEM, VMEM],
        out_specs=VMEM,
        scratch_shapes=[pltpu.VMEM((slot_total, LANES), f32)] + [field] * 4,
        compiler_params=params(),
        name="merge",
    )(cell, projected, arrived).reshape(height, width, LANES)

    around = [(i, (i + 1) % lon_size) for i in range(lon_size)]
    back = [(b, a) for a, b in around]
    left = lax.ppermute(merged[:, width - EDGE:], "lon", around)
    right = lax.ppermute(merged[:, :EDGE], "lon", back)
    down = [(i, i + 1) for i in range(lat_size - 1)]
    up = [(b, a) for a, b in down]

    def strip(at):
        return jnp.concatenate([left[at], merged[at], right[at]], axis=1)

    top = lax.ppermute(strip(slice(height - 2, height)), "lat", down)
    bottom = lax.ppermute(strip(slice(0, 2)), "lat", up)
    me = lax.axis_index("lat")
    ends = jnp.stack([(me == 0).astype(jnp.int32), (me == lat_size - 1).astype(jnp.int32)])

    corrected, picked = pl.pallas_call(
        functools.partial(conv_kernel, features),
        out_shape=(
            jax.ShapeDtypeStruct((height, features, width), bf16),
            jax.ShapeDtypeStruct((slot_total, LANES), bf16),
        ),
        in_specs=[SMEM, SMEM] + [VMEM] * 9,
        out_specs=(VMEM, VMEM),
        scratch_shapes=[
            pltpu.VMEM((height + 4, 3, width + EDGE, LANES), bf16),
            pltpu.VMEM((width + 2 * EDGE, LANES), f32),
            pltpu.VMEM((cells, LANES), f32),
            pltpu.VMEM((slot_total, LANES), f32),
        ],
        compiler_params=params(),
        name="convs",
    )(
        ends,
        cell,
        merged,
        left,
        right,
        top,
        bottom,
        pair_weights(initial_filter_matrix),
        pair_bias(initial_filter_offset),
        pair_weights(latter_filter_matrix),
        pair_bias(latter_filter_offset),
    )

    station_values = pl.pallas_call(
        functools.partial(return_kernel, features),
        out_shape=jax.ShapeDtypeStruct((held_rows, features), bf16),
        in_specs=[SMEM, VMEM],
        out_specs=VMEM,
        scratch_shapes=[
            pltpu.VMEM((slot_total, LANES), f32),
            pltpu.VMEM((held_rows, LANES), f32),
        ],
        compiler_params=params(),
        name="unroute",
    )(position, exchange(picked))
    return (jnp.transpose(corrected, (1, 0, 2)), station_values)


def solution(mesh):
    placed = (
        P(None, "lat", "lon"),
        P(),
        P(),
        P(("lon", "lat"), None),
        P(),
        P(),
        P(("lon", "lat"), None),
        P(("lon", "lat")),
        P(),
        P(),
        P(),
        P(),
    )
    return jax.shard_map(
        on_device,
        mesh=mesh,
        in_specs=placed,
        out_specs=(P(None, "lat", "lon"), P(("lon", "lat"), None)),
        check_vma=False,
    )
```

```python
import functools

import jax
import jax.numpy as jnp
from jax import lax
from jax.experimental import pallas as pl
from jax.experimental.pallas import tpu as pltpu
from jax.sharding import PartitionSpec as P

LANES = 128
EDGE = 16
VMEM_BYTES = 56 * 1024 * 1024

VMEM = pl.BlockSpec(memory_space=pltpu.VMEM)
SMEM = pl.BlockSpec(memory_space=pltpu.SMEM)


def params():
    return pltpu.CompilerParams(vmem_limit_bytes=VMEM_BYTES)


def turned(rows, d, capacity, kept):
    at = pl.ds(pl.multiple_of(d * capacity, 16), capacity)
    return rows[at, :].T[:kept].astype(jnp.bfloat16)


def turn_back(rows, got_ref):
    devices, kept, capacity = got_ref.shape

    @pl.loop(0, devices)
    def _(d):
        block = got_ref[d].astype(jnp.float32)
        block = jnp.concatenate([block, jnp.zeros((LANES - kept, capacity), jnp.float32)], axis=0)
        rows[pl.ds(pl.multiple_of(d * capacity, 16), capacity), :] = block.T


def route_kernel(features, columns, pos_ref, cell_ref, rec_ref, w_ref, off_ref, out_ref, emb, slots):
    rows = rec_ref.shape[0]
    devices, sent, capacity = out_ref.shape
    total = devices * capacity

    @pl.loop(0, total // 128)
    def _(b):
        slots[pl.ds(pl.multiple_of(b * 128, 128), 128), :] = jnp.zeros((128, LANES), jnp.float32)

    lane = lax.broadcasted_iota(jnp.int32, (128, LANES), 1)

    @pl.loop(0, rows // 128)
    def _(b):
        at = pl.ds(pl.multiple_of(b * 128, 128), 128)
        e = jnp.dot(rec_ref[at, :], w_ref[...], preferred_element_type=jnp.float32) + off_ref[...]
        e = e.astype(jnp.bfloat16).astype(jnp.float32)
        cell = jnp.broadcast_to(cell_ref[pl.ds(b, 1), :], (128, 128)).T
        line = (cell // columns + 1).astype(jnp.float32)
        place = (cell % columns).astype(jnp.float32)
        e = jnp.where(lane == features, line, jnp.where(lane == features + 1, place, e))
        emb[at, :] = e

    @pl.loop(0, rows // 16)
    def _(b):
        for j in range(16):
            i = b * 16 + j
            slots[pl.ds(pos_ref[i], 1), :] = emb[pl.ds(i, 1), :]

    @pl.loop(0, devices)
    def _(d):
        out_ref[d] = turned(slots, d, capacity, sent)


def merge_kernel(cell_ref, proj_ref, arr_ref, out_ref, rows32, s1, s2, s3, s0):
    total = rows32.shape[0]
    cells = proj_ref.shape[0]
    turn_back(rows32, arr_ref)

    @pl.loop(0, cells // 128)
    def _(b):
        at = pl.ds(pl.multiple_of(b * 128, 128), 128)
        for s in (s0, s1, s2, s3):
            s[at, :] = jnp.zeros((128, LANES), jnp.float32)

    sums = (s0, s1, s2, s3)

    @pl.loop(0, total // 16)
    def _(b):
        for g in range(4):
            idx = [b * 16 + g * 4 + j for j in range(4)]
            at = [pl.ds(cell_ref[i], 1) for i in idx]
            new = [sums[j][at[j], :] + rows32[pl.ds(idx[j], 1), :] for j in range(4)]
            for j in range(4):
                sums[j][at[j], :] = new[j]

    @pl.loop(0, cells // 128)
    def _(b):
        at = pl.ds(pl.multiple_of(b * 128, 128), 128)
        out_ref[at, :] = (
            proj_ref[at, :] + ((s0[at, :] + s1[at, :]) + (s2[at, :] + s3[at, :]))
        ).astype(jnp.bfloat16)


def pair_dot(patches, row, width, w_ref):
    lhs = jnp.concatenate(
        [patches[row + dr, k, pl.ds(0, width), :] for dr in range(4) for k in range(3)], axis=1
    )
    return jnp.dot(lhs, w_ref[...], preferred_element_type=jnp.float32)


def halo_kernel(
    lon_size, lat_size, m_ref, left_ref, right_ref, top_ref, bottom_ref, send_sem, recv_sem
):
    height, width, _ = m_ref.shape
    lon, lat = lax.axis_index("lon"), lax.axis_index("lat")
    ways = [(a, b) for a in (-1, 0, 1) for b in (-1, 0, 1) if (a, b) != (0, 0)]

    def there(a, b):
        return (lax.rem(lon + a + lon_size, lon_size), lax.rem(lat + b + lat_size, lat_size))

    barrier = pltpu.get_barrier_semaphore()
    for a, b in ways:
        pl.semaphore_signal(
            barrier, inc=1, device_id=there(a, b), device_id_type=pl.DeviceIdType.MESH
        )
    pl.semaphore_wait(barrier, len(ways))

    from_columns = {1: pl.ds(width - EDGE, EDGE), 0: pl.ds(0, width), -1: pl.ds(0, EDGE)}
    to_columns = {1: pl.ds(0, EDGE), 0: pl.ds(EDGE, width), -1: pl.ds(EDGE + width, EDGE)}
    from_rows = {1: pl.ds(height - 2, 2), 0: pl.ds(0, height), -1: pl.ds(0, 2)}
    copies = []
    for n, (a, b) in enumerate(ways):
        if b == 0:
            target = left_ref if a == 1 else right_ref
        else:
            target = (top_ref if b == 1 else bottom_ref).at[:, to_columns[a], :]
        copies.append(
            pltpu.make_async_remote_copy(
                src_ref=m_ref.at[from_rows[b], from_columns[a], :],
                dst_ref=target,
                send_sem=send_sem.at[n],
                recv_sem=recv_sem.at[n],
                device_id=there(a, b),
                device_id_type=pl.DeviceIdType.MESH,
            )
        )
    for copy in copies:
        copy.start()
    for copy in copies:
        copy.wait()


def conv_kernel(
    features, ends_ref, cell_ref, m_ref, left_ref, right_ref, top_ref, bottom_ref,
    w1_ref, b1_ref, w2_ref, b2_ref, out_ref, got_ref, patches, wide, corr, stage,
):
    height, width, _ = m_ref.shape
    tall = width + EDGE

    def spread(row):
        for k in range(3):
            patches[row, k, :, :] = wide[pl.ds(EDGE - 2 + k, tall), :].astype(jnp.bfloat16)

    for n, ref, base in ((0, top_ref, 0), (1, bottom_ref, height + 2)):
        for t in range(2):
            wide[...] = jnp.where(ends_ref[n] == 1, 0.0, ref[t].astype(jnp.float32))
            spread(base + t)

    @pl.loop(0, height)
    def _(r):
        wide[pl.ds(0, EDGE), :] = left_ref[r].astype(jnp.float32)
        wide[pl.ds(EDGE, width), :] = m_ref[r].astype(jnp.float32)
        wide[pl.ds(EDGE + width, EDGE), :] = right_ref[r].astype(jnp.float32)
        spread(r + 2)

    @pl.loop(0, height // 2 + 1)
    def _(p):
        y = pair_dot(patches, 2 * p, tall, w1_ref) + b1_ref[...]
        hidden = jax.nn.gelu(y)
        for t in range(2):
            h = 2 * p + t
            outside = ((h == 0) & (ends_ref[0] == 1)) | ((h == height + 1) & (ends_ref[1] == 1))
            part = hidden[:, t * LANES:(t + 1) * LANES]
            wide[pl.ds(0, tall), :] = jnp.where(outside, 0.0, part)
            for k in range(3):
                patches[h, k, pl.ds(0, width), :] = wide[pl.ds(k, width), :].astype(jnp.bfloat16)

    @pl.loop(0, height // 2)
    def _(p):
        y = pair_dot(patches, 2 * p, width, w2_ref) + b2_ref[...]
        for t in range(2):
            r = 2 * p + t
            v = m_ref[r].astype(jnp.float32) + y[:, t * LANES:(t + 1) * LANES]
            corr[pl.ds(pl.multiple_of(r * width, 128), width), :] = v
            out_ref[r] = v.T[:features].astype(jnp.bfloat16)

    devices, kept, capacity = got_ref.shape

    @pl.loop(0, devices * capacity // 16)
    def _(b):
        for j in range(16):
            i = b * 16 + j
            stage[pl.ds(i, 1), :] = corr[pl.ds(cell_ref[i], 1), :]

    @pl.loop(0, devices)
    def _(d):
        got_ref[d] = turned(stage, d, capacity, kept)


def return_kernel(features, pos_ref, got_ref, out_ref, rows32, stage):
    rows = out_ref.shape[1]
    turn_back(rows32, got_ref)

    @pl.loop(0, rows // 16)
    def _(b):
        for j in range(16):
            i = b * 16 + j
            stage[pl.ds(i, 1), :] = rows32[pl.ds(pos_ref[i], 1), :]

    @pl.loop(0, rows // 128)
    def _(b):
        at = pl.ds(pl.multiple_of(b * 128, 128), 128)
        out_ref[:, at] = stage[at, :].T[:features].astype(jnp.bfloat16)


def slots_of(tile, devices, capacity):
    block = 128
    hot = (tile.reshape(-1, block)[:, :, None] == jnp.arange(devices, dtype=jnp.int32)).astype(
        jnp.bfloat16
    )
    below = jnp.tril(jnp.ones((block, block), jnp.bfloat16), -1)
    inside = jnp.einsum("ij,bjd->bid", below, hot, preferred_element_type=jnp.float32)
    totals = jnp.sum(hot.astype(jnp.float32), axis=1)
    blocks = totals.shape[0]
    before = jnp.sum(
        jnp.where(
            (jnp.arange(blocks)[:, None] > jnp.arange(blocks)[None, :])[:, :, None],
            totals[None],
            0.0,
        ),
        axis=1,
    )
    rank = jnp.sum((inside + before[:, None, :]) * hot.astype(jnp.float32), axis=2)
    return tile * capacity + rank.reshape(-1).astype(jnp.int32)


def pair_weights(kernel):
    out, into = kernel.shape[:2]
    k = jnp.pad(
        jnp.transpose(kernel, (2, 3, 1, 0)), ((0, 0), (0, 0), (0, LANES - into), (0, LANES - out))
    )
    rest = ((0, 0), (0, 0), (0, 0))
    both = jnp.concatenate(
        [jnp.pad(k, ((0, 1),) + rest), jnp.pad(k, ((1, 0),) + rest)], axis=3
    )
    return both.reshape(4 * 3 * LANES, 2 * LANES)


def pair_bias(bias):
    padded = jnp.pad(bias, (0, LANES - bias.shape[0]))
    return jnp.concatenate([padded, padded])[None]


def on_device(
    ensemble_prediction,
    mapping_matrix,
    mapping_offset,
    gauge_measured_records,
    gauge_scatter_matrix,
    gauge_scatter_offset,
    gauge_block_number,
    gauge_point_position,
    initial_filter_matrix,
    initial_filter_offset,
    latter_filter_matrix,
    latter_filter_offset,
):
    depth, height, width = ensemble_prediction.shape
    features = mapping_matrix.shape[0]
    more = LANES - features
    cells = height * width
    lon_size = lax.axis_size("lon")
    lat_size = lax.axis_size("lat")
    devices = lon_size * lat_size
    held_rows = gauge_measured_records.shape[0]
    capacity = 2 * held_rows // devices
    slot_total = devices * capacity
    f32, bf16 = jnp.float32, jnp.bfloat16

    def exchange(rows):
        return lax.all_to_all(
            rows,
            ("lon", "lat"),
            split_axis=0,
            concat_axis=0,
            tiled=True,
        )

    position = slots_of(gauge_block_number[:, 0], devices, capacity)
    payload = pl.pallas_call(
        functools.partial(route_kernel, features, width),
        out_shape=jax.ShapeDtypeStruct((devices, features + 8, capacity), bf16),
        in_specs=[SMEM, VMEM, VMEM, VMEM, VMEM],
        out_specs=VMEM,
        scratch_shapes=[
            pltpu.VMEM((held_rows, LANES), f32),
            pltpu.VMEM((slot_total, LANES), f32),
        ],
        compiler_params=params(),
        name="route",
    )(
        position,
        gauge_point_position.reshape(-1, 128),
        gauge_measured_records,
        jnp.pad(gauge_scatter_matrix, ((0, 0), (0, more))),
        jnp.pad(gauge_scatter_offset, (0, more))[None],
    )
    arrived = exchange(payload)
    line = arrived[:, features].astype(jnp.int32).reshape(slot_total)
    place = arrived[:, features + 1].astype(jnp.int32).reshape(slot_total)
    cell = jnp.clip((line - 1) * width + place, 0, cells - 1)

    projected = lax.dot_general(
        ensemble_prediction.reshape(depth, cells),
        jnp.pad(mapping_matrix, ((0, more), (0, 0))),
        (((0,), (1,)), ((), ())),
        preferred_element_type=f32,
    ) + jnp.pad(mapping_offset, (0, more))[None]

    field = pltpu.VMEM((cells, LANES), f32)
    merged = pl.pallas_call(
        merge_kernel,
        out_shape=jax.ShapeDtypeStruct((cells, LANES), bf16),
        in_specs=[SMEM, VMEM, VMEM],
        out_specs=VMEM,
        scratch_shapes=[pltpu.VMEM((slot_total, LANES), f32)] + [field] * 4,
        compiler_params=params(),
        name="merge",
    )(cell, projected, arrived).reshape(height, width, LANES)

    side = jax.ShapeDtypeStruct((height, EDGE, LANES), bf16)
    strip = jax.ShapeDtypeStruct((2, width + 2 * EDGE, LANES), bf16)
    anywhere = pl.BlockSpec(memory_space=pl.ANY)
    left, right, top, bottom = pl.pallas_call(
        functools.partial(halo_kernel, lon_size, lat_size),
        out_shape=(side, side, strip, strip),
        in_specs=[anywhere],
        out_specs=(anywhere,) * 4,
        scratch_shapes=[pltpu.SemaphoreType.DMA((8,)), pltpu.SemaphoreType.DMA((8,))],
        compiler_params=pltpu.CompilerParams(collective_id=0, has_side_effects=True),
        name="halo",
    )(merged)
    me = lax.axis_index("lat")
    ends = jnp.stack([(me == 0).astype(jnp.int32), (me == lat_size - 1).astype(jnp.int32)])

    corrected, picked = pl.pallas_call(
        functools.partial(conv_kernel, features),
        out_shape=(
            jax.ShapeDtypeStruct((height, features, width), bf16),
            jax.ShapeDtypeStruct((devices, features, capacity), bf16),
        ),
        in_specs=[SMEM, SMEM] + [VMEM] * 9,
        out_specs=(VMEM, VMEM),
        scratch_shapes=[
            pltpu.VMEM((height + 4, 3, width + EDGE, LANES), bf16),
            pltpu.VMEM((width + 2 * EDGE, LANES), f32),
            pltpu.VMEM((cells, LANES), f32),
            pltpu.VMEM((slot_total, LANES), f32),
        ],
        compiler_params=params(),
        name="convs",
    )(
        ends,
        cell,
        merged,
        left,
        right,
        top,
        bottom,
        pair_weights(initial_filter_matrix),
        pair_bias(initial_filter_offset),
        pair_weights(latter_filter_matrix),
        pair_bias(latter_filter_offset),
    )

    station_values = pl.pallas_call(
        functools.partial(return_kernel, features),
        out_shape=jax.ShapeDtypeStruct((features, held_rows), bf16),
        in_specs=[SMEM, VMEM],
        out_specs=VMEM,
        scratch_shapes=[
            pltpu.VMEM((slot_total, LANES), f32),
            pltpu.VMEM((held_rows, LANES), f32),
        ],
        compiler_params=params(),
        name="unroute",
    )(position, exchange(picked))
    return (jnp.transpose(corrected, (1, 0, 2)), station_values.T)


def solution(mesh):
    placed = (
        P(None, "lat", "lon"),
        P(),
        P(),
        P(("lon", "lat"), None),
        P(),
        P(),
        P(("lon", "lat"), None),
        P(("lon", "lat")),
        P(),
        P(),
        P(),
        P(),
    )
    return jax.shard_map(
        on_device,
        mesh=mesh,
        in_specs=placed,
        out_specs=(P(None, "lat", "lon"), P(("lon", "lat"), None)),
        check_vma=False,
    )
```

```python
import functools

import jax
import jax.numpy as jnp
from jax import lax
from jax.experimental import pallas as pl
from jax.experimental.pallas import tpu as pltpu
from jax.sharding import PartitionSpec as P

LANES = 128
EDGE = 16
VMEM_BYTES = 56 * 1024 * 1024

VMEM = pl.BlockSpec(memory_space=pltpu.VMEM)
SMEM = pl.BlockSpec(memory_space=pltpu.SMEM)


def params():
    return pltpu.CompilerParams(vmem_limit_bytes=VMEM_BYTES)


def turned(rows, d, capacity, kept):
    at = pl.ds(pl.multiple_of(d * capacity, 16), capacity)
    return rows[at, :].T[:kept].astype(jnp.bfloat16)


def turn_back(rows, got_ref):
    devices, kept, capacity = got_ref.shape

    @pl.loop(0, devices, unroll=4)
    def _(d):
        block = got_ref[d].astype(jnp.float32)
        block = jnp.concatenate([block, jnp.zeros((LANES - kept, capacity), jnp.float32)], axis=0)
        rows[pl.ds(pl.multiple_of(d * capacity, 16), capacity), :] = block.T


def route_kernel(features, columns, pos_ref, cell_ref, rec_ref, w_ref, off_ref, out_ref, emb, slots):
    rows = rec_ref.shape[0]
    devices, sent, capacity = out_ref.shape
    total = devices * capacity

    @pl.loop(0, total // 128, unroll=4)
    def _(b):
        slots[pl.ds(pl.multiple_of(b * 128, 128), 128), :] = jnp.zeros((128, LANES), jnp.float32)

    lane = lax.broadcasted_iota(jnp.int32, (128, LANES), 1)

    @pl.loop(0, rows // 128, unroll=4)
    def _(b):
        at = pl.ds(pl.multiple_of(b * 128, 128), 128)
        e = jnp.dot(rec_ref[at, :], w_ref[...], preferred_element_type=jnp.float32) + off_ref[...]
        e = e.astype(jnp.bfloat16).astype(jnp.float32)
        cell = jnp.broadcast_to(cell_ref[pl.ds(b, 1), :], (128, 128)).T
        line = (cell // columns + 1).astype(jnp.float32)
        place = (cell % columns).astype(jnp.float32)
        e = jnp.where(lane == features, line, jnp.where(lane == features + 1, place, e))
        emb[at, :] = e

    @pl.loop(0, rows // 16)
    def _(b):
        for j in range(16):
            i = b * 16 + j
            slots[pl.ds(pos_ref[i], 1), :] = emb[pl.ds(i, 1), :]

    @pl.loop(0, devices, unroll=4)
    def _(d):
        out_ref[d] = turned(slots, d, capacity, sent)


def merge_kernel(cell_ref, proj_ref, arr_ref, out_ref, rows32, s1, s2, s3, s0):
    total = rows32.shape[0]
    cells = proj_ref.shape[0]
    turn_back(rows32, arr_ref)

    @pl.loop(0, cells // 128, unroll=4)
    def _(b):
        at = pl.ds(pl.multiple_of(b * 128, 128), 128)
        for s in (s0, s1, s2, s3):
            s[at, :] = jnp.zeros((128, LANES), jnp.float32)

    sums = (s0, s1, s2, s3)

    @pl.loop(0, total // 16)
    def _(b):
        for g in range(4):
            idx = [b * 16 + g * 4 + j for j in range(4)]
            at = [pl.ds(cell_ref[i], 1) for i in idx]
            new = [sums[j][at[j], :] + rows32[pl.ds(idx[j], 1), :] for j in range(4)]
            for j in range(4):
                sums[j][at[j], :] = new[j]

    @pl.loop(0, cells // 128, unroll=4)
    def _(b):
        at = pl.ds(pl.multiple_of(b * 128, 128), 128)
        out_ref[at, :] = (
            proj_ref[at, :] + ((s0[at, :] + s1[at, :]) + (s2[at, :] + s3[at, :]))
        ).astype(jnp.bfloat16)


def pair_dot(patches, row, width, w_ref):
    lhs = jnp.concatenate(
        [patches[row + dr, k, pl.ds(0, width), :] for dr in range(4) for k in range(3)], axis=1
    )
    return jnp.dot(lhs, w_ref[...], preferred_element_type=jnp.float32)


def halo_kernel(
    lon_size, lat_size, m_ref, left_ref, right_ref, top_ref, bottom_ref, send_sem, recv_sem
):
    height, width, _ = m_ref.shape
    lon, lat = lax.axis_index("lon"), lax.axis_index("lat")
    ways = [(a, b) for a in (-1, 0, 1) for b in (-1, 0, 1) if (a, b) != (0, 0)]

    def there(a, b):
        return (lax.rem(lon + a + lon_size, lon_size), lax.rem(lat + b + lat_size, lat_size))

    barrier = pltpu.get_barrier_semaphore()
    for a, b in ways:
        pl.semaphore_signal(
            barrier, inc=1, device_id=there(a, b), device_id_type=pl.DeviceIdType.MESH
        )
    pl.semaphore_wait(barrier, len(ways))

    from_columns = {1: pl.ds(width - EDGE, EDGE), 0: pl.ds(0, width), -1: pl.ds(0, EDGE)}
    to_columns = {1: pl.ds(0, EDGE), 0: pl.ds(EDGE, width), -1: pl.ds(EDGE + width, EDGE)}
    from_rows = {1: pl.ds(height - 2, 2), 0: pl.ds(0, height), -1: pl.ds(0, 2)}
    copies = []
    for n, (a, b) in enumerate(ways):
        if b == 0:
            target = left_ref if a == 1 else right_ref
        else:
            target = (top_ref if b == 1 else bottom_ref).at[:, to_columns[a], :]
        copies.append(
            pltpu.make_async_remote_copy(
                src_ref=m_ref.at[from_rows[b], from_columns[a], :],
                dst_ref=target,
                send_sem=send_sem.at[n],
                recv_sem=recv_sem.at[n],
                device_id=there(a, b),
                device_id_type=pl.DeviceIdType.MESH,
            )
        )
    for copy in copies:
        copy.start()
    for copy in copies:
        copy.wait()


def conv_kernel(
    features, ends_ref, cell_ref, m_ref, left_ref, right_ref, top_ref, bottom_ref,
    w1_ref, b1_ref, w2_ref, b2_ref, out_ref, got_ref, patches, wide, corr, stage,
):
    height, width, _ = m_ref.shape
    tall = width + EDGE

    def spread(row):
        for k in range(3):
            patches[row, k, :, :] = wide[pl.ds(EDGE - 2 + k, tall), :].astype(jnp.bfloat16)

    for n, ref, base in ((0, top_ref, 0), (1, bottom_ref, height + 2)):
        for t in range(2):
            wide[...] = jnp.where(ends_ref[n] == 1, 0.0, ref[t].astype(jnp.float32))
            spread(base + t)

    @pl.loop(0, height, unroll=2)
    def _(r):
        wide[pl.ds(0, EDGE), :] = left_ref[r].astype(jnp.float32)
        wide[pl.ds(EDGE, width), :] = m_ref[r].astype(jnp.float32)
        wide[pl.ds(EDGE + width, EDGE), :] = right_ref[r].astype(jnp.float32)
        spread(r + 2)

    @pl.loop(0, height // 2 + 1, unroll=3)
    def _(p):
        y = pair_dot(patches, 2 * p, tall, w1_ref) + b1_ref[...]
        hidden = jax.nn.gelu(y)
        for t in range(2):
            h = 2 * p + t
            outside = ((h == 0) & (ends_ref[0] == 1)) | ((h == height + 1) & (ends_ref[1] == 1))
            part = hidden[:, t * LANES:(t + 1) * LANES]
            wide[pl.ds(0, tall), :] = jnp.where(outside, 0.0, part)
            for k in range(3):
                patches[h, k, pl.ds(0, width), :] = wide[pl.ds(k, width), :].astype(jnp.bfloat16)

    @pl.loop(0, height // 2, unroll=2)
    def _(p):
        y = pair_dot(patches, 2 * p, width, w2_ref) + b2_ref[...]
        for t in range(2):
            r = 2 * p + t
            v = m_ref[r].astype(jnp.float32) + y[:, t * LANES:(t + 1) * LANES]
            corr[pl.ds(pl.multiple_of(r * width, 128), width), :] = v
            out_ref[r] = v.T[:features].astype(jnp.bfloat16)

    devices, kept, capacity = got_ref.shape

    @pl.loop(0, devices * capacity // 16)
    def _(b):
        for j in range(16):
            i = b * 16 + j
            stage[pl.ds(i, 1), :] = corr[pl.ds(cell_ref[i], 1), :]

    @pl.loop(0, devices, unroll=4)
    def _(d):
        got_ref[d] = turned(stage, d, capacity, kept)


def return_kernel(features, pos_ref, got_ref, out_ref, rows32, stage):
    rows = out_ref.shape[1]
    turn_back(rows32, got_ref)

    @pl.loop(0, rows // 16)
    def _(b):
        for j in range(16):
            i = b * 16 + j
            stage[pl.ds(i, 1), :] = rows32[pl.ds(pos_ref[i], 1), :]

    @pl.loop(0, rows // 128, unroll=4)
    def _(b):
        at = pl.ds(pl.multiple_of(b * 128, 128), 128)
        out_ref[:, at] = stage[at, :].T[:features].astype(jnp.bfloat16)


def slots_of(tile, devices, capacity):
    block = 128
    hot = (tile.reshape(-1, block)[:, :, None] == jnp.arange(devices, dtype=jnp.int32)).astype(
        jnp.bfloat16
    )
    below = jnp.tril(jnp.ones((block, block), jnp.bfloat16), -1)
    inside = jnp.einsum("ij,bjd->bid", below, hot, preferred_element_type=jnp.float32)
    totals = jnp.sum(hot.astype(jnp.float32), axis=1)
    blocks = totals.shape[0]
    before = jnp.sum(
        jnp.where(
            (jnp.arange(blocks)[:, None] > jnp.arange(blocks)[None, :])[:, :, None],
            totals[None],
            0.0,
        ),
        axis=1,
    )
    rank = jnp.sum((inside + before[:, None, :]) * hot.astype(jnp.float32), axis=2)
    return tile * capacity + rank.reshape(-1).astype(jnp.int32)


def pair_weights(kernel):
    out, into = kernel.shape[:2]
    k = jnp.pad(
        jnp.transpose(kernel, (2, 3, 1, 0)), ((0, 0), (0, 0), (0, LANES - into), (0, LANES - out))
    )
    rest = ((0, 0), (0, 0), (0, 0))
    both = jnp.concatenate(
        [jnp.pad(k, ((0, 1),) + rest), jnp.pad(k, ((1, 0),) + rest)], axis=3
    )
    return both.reshape(4 * 3 * LANES, 2 * LANES)


def pair_bias(bias):
    padded = jnp.pad(bias, (0, LANES - bias.shape[0]))
    return jnp.concatenate([padded, padded])[None]


def on_device(
    ensemble_prediction,
    mapping_matrix,
    mapping_offset,
    gauge_measured_records,
    gauge_scatter_matrix,
    gauge_scatter_offset,
    gauge_block_number,
    gauge_point_position,
    initial_filter_matrix,
    initial_filter_offset,
    latter_filter_matrix,
    latter_filter_offset,
):
    depth, height, width = ensemble_prediction.shape
    features = mapping_matrix.shape[0]
    more = LANES - features
    cells = height * width
    lon_size = lax.axis_size("lon")
    lat_size = lax.axis_size("lat")
    devices = lon_size * lat_size
    held_rows = gauge_measured_records.shape[0]
    capacity = 2 * held_rows // devices
    slot_total = devices * capacity
    f32, bf16 = jnp.float32, jnp.bfloat16

    def exchange(rows):
        return lax.all_to_all(
            rows,
            ("lon", "lat"),
            split_axis=0,
            concat_axis=0,
            tiled=True,
        )

    position = slots_of(gauge_block_number[:, 0], devices, capacity)
    payload = pl.pallas_call(
        functools.partial(route_kernel, features, width),
        out_shape=jax.ShapeDtypeStruct((devices, features + 8, capacity), bf16),
        in_specs=[SMEM, VMEM, VMEM, VMEM, VMEM],
        out_specs=VMEM,
        scratch_shapes=[
            pltpu.VMEM((held_rows, LANES), f32),
            pltpu.VMEM((slot_total, LANES), f32),
        ],
        compiler_params=params(),
        name="route",
    )(
        position,
        gauge_point_position.reshape(-1, 128),
        gauge_measured_records,
        jnp.pad(gauge_scatter_matrix, ((0, 0), (0, more))),
        jnp.pad(gauge_scatter_offset, (0, more))[None],
    )
    arrived = exchange(payload)
    line = arrived[:, features].astype(jnp.int32).reshape(slot_total)
    place = arrived[:, features + 1].astype(jnp.int32).reshape(slot_total)
    cell = jnp.clip((line - 1) * width + place, 0, cells - 1)

    projected = lax.dot_general(
        ensemble_prediction.reshape(depth, cells),
        jnp.pad(mapping_matrix, ((0, more), (0, 0))),
        (((0,), (1,)), ((), ())),
        preferred_element_type=f32,
    ) + jnp.pad(mapping_offset, (0, more))[None]

    field = pltpu.VMEM((cells, LANES), f32)
    merged = pl.pallas_call(
        merge_kernel,
        out_shape=jax.ShapeDtypeStruct((cells, LANES), bf16),
        in_specs=[SMEM, VMEM, VMEM],
        out_specs=VMEM,
        scratch_shapes=[pltpu.VMEM((slot_total, LANES), f32)] + [field] * 4,
        compiler_params=params(),
        name="merge",
    )(cell, projected, arrived).reshape(height, width, LANES)

    side = jax.ShapeDtypeStruct((height, EDGE, LANES), bf16)
    strip = jax.ShapeDtypeStruct((2, width + 2 * EDGE, LANES), bf16)
    anywhere = pl.BlockSpec(memory_space=pl.ANY)
    left, right, top, bottom = pl.pallas_call(
        functools.partial(halo_kernel, lon_size, lat_size),
        out_shape=(side, side, strip, strip),
        in_specs=[anywhere],
        out_specs=(anywhere,) * 4,
        scratch_shapes=[pltpu.SemaphoreType.DMA((8,)), pltpu.SemaphoreType.DMA((8,))],
        compiler_params=pltpu.CompilerParams(collective_id=0, has_side_effects=True),
        name="halo",
    )(merged)
    me = lax.axis_index("lat")
    ends = jnp.stack([(me == 0).astype(jnp.int32), (me == lat_size - 1).astype(jnp.int32)])

    corrected, picked = pl.pallas_call(
        functools.partial(conv_kernel, features),
        out_shape=(
            jax.ShapeDtypeStruct((height, features, width), bf16),
            jax.ShapeDtypeStruct((devices, features, capacity), bf16),
        ),
        in_specs=[SMEM, SMEM] + [VMEM] * 9,
        out_specs=(VMEM, VMEM),
        scratch_shapes=[
            pltpu.VMEM((height + 4, 3, width + EDGE, LANES), bf16),
            pltpu.VMEM((width + 2 * EDGE, LANES), f32),
            pltpu.VMEM((cells, LANES), f32),
            pltpu.VMEM((slot_total, LANES), f32),
        ],
        compiler_params=params(),
        name="convs",
    )(
        ends,
        cell,
        merged,
        left,
        right,
        top,
        bottom,
        pair_weights(initial_filter_matrix),
        pair_bias(initial_filter_offset),
        pair_weights(latter_filter_matrix),
        pair_bias(latter_filter_offset),
    )

    station_values = pl.pallas_call(
        functools.partial(return_kernel, features),
        out_shape=jax.ShapeDtypeStruct((features, held_rows), bf16),
        in_specs=[SMEM, VMEM],
        out_specs=VMEM,
        scratch_shapes=[
            pltpu.VMEM((slot_total, LANES), f32),
            pltpu.VMEM((held_rows, LANES), f32),
        ],
        compiler_params=params(),
        name="unroute",
    )(position, exchange(picked))
    return (jnp.transpose(corrected, (1, 0, 2)), station_values.T)


def solution(mesh):
    placed = (
        P(None, "lat", "lon"),
        P(),
        P(),
        P(("lon", "lat"), None),
        P(),
        P(),
        P(("lon", "lat"), None),
        P(("lon", "lat")),
        P(),
        P(),
        P(),
        P(),
    )
    return jax.shard_map(
        on_device,
        mesh=mesh,
        in_specs=placed,
        out_specs=(P(None, "lat", "lon"), P(("lon", "lat"), None)),
        check_vma=False,
    )
```
